32 devices in a mesh: lat: 4 (over x, core), lon: 8 (over z, y).
Axes of the slice: x: 2, y: 2, z: 4, core: 2. Of those that a mesh axis runs over, the one named last changes fastest.
Arguments:
- grad_out: bfloat16 [704, 1440, 256], P('lat', 'lon'), may hold values from -6 to 6
- block_input: bfloat16 [704, 1440, 256], P('lat', 'lon'), may hold values from -6 to 6
- leg_table: bfloat16 [384, 384, 704], P('lat'), may hold values from -1 to 1, as said below
- spec_coeff: bfloat16 [384, 384, 2, 256], P(None, 'lat', None, 'lon'), may hold values from -6 to 6
- spec_filter: float32 [384, 256], P(None, 'lon'), may hold values from -6 to 6
- cycle_weight: float32 [704, 3], replicated, may hold values from 0.2 to 2
- cycle_shift: int32 [704, 3], replicated, may hold values from -1 to 1
- tap_weight: bfloat16 [3, 256, 256], replicated, may hold values from -0.21875 to 0.21875
Outputs:
- spec_grad: bfloat16 [384, 384, 2, 256], P(None, 'lat', None, 'lon')
- filter_grad: float32 [384, 256], P(None, 'lon')
- input_grad: bfloat16 [704, 1440, 256], P('lat', 'lon')
- taps_grad: float32 [3, 256, 256], replicated
The draws below stay inside these ranges and needn't reach their ends.
Inputs may be any that keep to these rules, and one draw needn't show every extreme that they name: `leg_table`: zero wherever the degree l is below the order m.
All inputs are finite; a program needn't handle non-finite values.
Results may differ from the reference program's by a relative error of at most 0.013.
Values may be sent and summed in bfloat16 or wider, within the bound.
A program may use at most 320 MiB of HBM per device.

```python
import math
import jax
import jax.numpy as jnp
from jax import lax

NLAT = 704
NLON = 1440
C = 256
MMAX = 384
LMAX = 384
TAPS = 3
N_LAT = 4


def draw_leg_table(key, part):
    base = jnp.clip(jax.random.normal(key, (MMAX, LMAX, NLAT), jnp.float32), -6.0, 6.0)
    keep = (jnp.arange(LMAX)[None, :, None] >= jnp.arange(MMAX)[:, None, None]).astype(jnp.float32)
    return (base * keep / math.sqrt(NLAT)).astype(jnp.bfloat16)


def plant(drawn, key, low, largest):
    place = [jax.random.randint(jax.random.fold_in(key, axis), (), 0, length) for axis, length in enumerate(drawn.shape)]
    longest = drawn.shape.index(max(drawn.shape))
    next_to = place[:longest] + [(place[longest] + 1) % drawn.shape[longest]] + place[longest + 1:]
    return drawn.at[tuple(place)].set(low).at[tuple(next_to)].set(largest)


def level_of(key, dims, cuts, low, high):
    def one(position, parts):
        draws = jax.random.uniform(jax.random.fold_in(jax.random.fold_in(key, 6), position), (parts,), jnp.float32, low / len(cuts), high / len(cuts))
        return jnp.repeat(jnp.exp(draws), dims[position] // parts).reshape((-1,) + (1,) * (len(dims) - position - 1))

    gain = one(*cuts[0])
    for cut in cuts[1:]:
        gain = gain * one(*cut)
    return gain


def bell_draw(stream_key, extent, width, most, cuts=(), kind=jnp.bfloat16):
    gain = level_of(stream_key, extent, cuts, -0.22, 0.18) if cuts else 1.0
    array = jax.random.normal(stream_key, extent, jnp.float32) * width * gain
    return jnp.minimum(jnp.maximum(array, -most), most).astype(kind)


def setup_inputs(seed: int = 0) -> dict:
    streams_of = jax.random.split(jax.random.key(seed), 9)
    grad_out = bell_draw(streams_of[0], (NLAT, NLON, C), 1.0, 6.0, ((0, 4), (1, 8)))
    block_input = bell_draw(streams_of[1], (NLAT, NLON, C), 1.0, 6.0, ((0, 4), (1, 8)))
    leg_table = draw_leg_table(jax.random.fold_in(streams_of[8], 71), 0)
    spec_coeff = bell_draw(streams_of[3], (LMAX, MMAX, 2, C), 1.0, 6.0, ((1, 4), (3, 8)))
    spec_filter = bell_draw(streams_of[4], (LMAX, C), 1.0, 6.0, ((1, 8),), jnp.float32)
    cycle_weight = jnp.clip(jnp.exp(jax.random.uniform(streams_of[5], (NLAT, TAPS), jnp.float32, math.log(0.2), math.log(2.0))), 0.2, 2.0)
    cycle_shift = plant(jax.random.randint(streams_of[6], (NLAT, TAPS), -1, 2), jax.random.fold_in(streams_of[6], 1), -1, 1).astype(jnp.int32)
    tap_weight = bell_draw(streams_of[7], (TAPS, C, C), (TAPS * C) ** -0.5, 0.21875)
    return {"grad_out": grad_out, "block_input": block_input, "leg_table": leg_table, "spec_coeff": spec_coeff, "spec_filter": spec_filter, "cycle_weight": cycle_weight, "cycle_shift": cycle_shift, "tap_weight": tap_weight}


def fourier_table(lon_count, mode_count):
    longitude = jnp.arange(lon_count, dtype=jnp.int32)[:, None]
    orders = jnp.arange(mode_count, dtype=jnp.int32)[None, :]
    phase = (longitude * orders % lon_count).astype(jnp.float32) * (2.0 * math.pi / lon_count)
    table = jnp.stack([jnp.cos(phase), jnp.sin(phase)], axis=-1) / math.sqrt(lon_count)
    return table.astype(jnp.bfloat16)

def reference(grad_out, block_input, leg_table, spec_coeff, spec_filter, cycle_weight, cycle_shift, tap_weight):
    table = fourier_table(NLON, MMAX).reshape(NLON, 2 * MMAX)
    table_rows = table.T

    def analyse(cycle):
        return jnp.dot(table_rows, cycle, preferred_element_type=jnp.float32)
    fourier = lax.map(analyse, grad_out).astype(jnp.bfloat16)
    by_order = jnp.moveaxis(fourier.reshape(NLAT, MMAX, 2 * C), 1, 0)

    def project(pair):
        return jnp.dot(pair[0], pair[1], preferred_element_type=jnp.float32)
    degree = lax.map(project, (leg_table, by_order))
    degree = jnp.transpose(degree.reshape(MMAX, LMAX, 2, C), (1, 0, 2, 3))
    spec_grad = (degree * spec_filter[:, None, None, :]).astype(jnp.bfloat16)
    filter_grad = lax.optimization_barrier(jnp.sum(spec_coeff.astype(jnp.float32) * degree, axis=(1, 2))) / math.sqrt(2 * MMAX)
    band = NLAT // N_LAT
    grad_pad = jnp.pad(grad_out, ((1, 1), (0, 0), (0, 0)))
    weight_pad = jnp.pad(cycle_weight, ((1, 1), (0, 0)))
    shift_pad = jnp.pad(cycle_shift, ((1, 1), (0, 0)))

    def band_step(total, band_index):
        start = (band_index * band).astype(jnp.int32)
        inputs = lax.dynamic_slice_in_dim(block_input, start, band, 0).reshape(-1, C)
        result = jnp.zeros((band * NLON, C), jnp.float32)
        for tap_index, offset in enumerate((-1, 0, 1)):
            source = lax.dynamic_slice_in_dim(grad_pad, start + 1 - offset, band, 0)
            coef = lax.dynamic_slice_in_dim(weight_pad, start + 1 - offset, band, 0)[:, tap_index]
            shifts = lax.dynamic_slice_in_dim(shift_pad, start + 1 - offset, band, 0)[:, tap_index]
            picked = jnp.zeros((band, NLON, C), jnp.float32)
            for column_shift in (-1, 0, 1):
                rolled = jnp.roll(source, column_shift, axis=1).astype(jnp.float32)
                picked = picked + (shifts == column_shift).astype(jnp.float32)[:, None, None] * rolled
            spread = (coef[:, None, None] * picked).astype(jnp.bfloat16).reshape(-1, C)
            result = result + lax.dot_general(spread, tap_weight[tap_index], (((1,), (1,)), ((), ())), preferred_element_type=jnp.float32)
            total = total.at[tap_index].add(lax.dot_general(inputs, spread, (((0,), (0,)), ((), ())), preferred_element_type=jnp.float32))
        return (total, result.reshape(band, NLON, C).astype(jnp.bfloat16))
    start_total = jnp.zeros((TAPS, C, C), jnp.float32)
    total, bands = lax.scan(band_step, start_total, jnp.arange(N_LAT, dtype=jnp.int32))
    input_grad = bands.reshape(NLAT, NLON, C)
    taps_grad = total / math.sqrt(NLAT * NLON)
    return (spec_grad, filter_grad, input_grad, taps_grad)
```

```python
import functools
import math

import jax
import jax.numpy as jnp
from jax import lax
from jax.experimental import pallas as pl
from jax.experimental.pallas import tpu as pltpu
from jax.sharding import PartitionSpec as P

VMEM_BYTES = 48 * 2**20


def largest_divisor(number, most):
    return max(d for d in range(1, most + 1) if number % d == 0)


def split_table(sectors, lons_here, mode_count):
    shape = (sectors, 2 * mode_count, lons_here)
    lon = lax.broadcasted_iota(jnp.int32, shape, 0) * lons_here + lax.broadcasted_iota(
        jnp.int32, shape, 2
    )
    row = lax.broadcasted_iota(jnp.int32, shape, 1)
    lon_count = sectors * lons_here
    phase = (lon * (row // 2) % lon_count).astype(jnp.float32) * (2.0 * math.pi / lon_count)
    value = jnp.where(row % 2 == 0, jnp.cos(phase), jnp.sin(phase)) / math.sqrt(lon_count)
    return value.astype(jnp.bfloat16)


def pack_kernel(groups, lanes, x_ref, out_ref):
    packs = x_ref.shape[1]
    for j in range(groups):
        parts = [x_ref[0, q, 0, :, j * lanes : (j + 1) * lanes] for q in range(packs)]
        out_ref[j, 0] = jnp.concatenate(parts, axis=-1)


def pack(field, chunk, groups):
    _, packs, slots, lons, channels = field.shape
    lanes = channels // groups
    return pl.pallas_call(
        functools.partial(pack_kernel, groups, lanes),
        grid=(slots,),
        in_specs=[pl.BlockSpec((1, packs, 1, lons, channels), lambda s: (chunk, 0, s, 0, 0))],
        out_specs=pl.BlockSpec((groups, 1, lons, packs * lanes), lambda s: (0, s, 0, 0)),
        out_shape=jax.ShapeDtypeStruct((groups, slots, lons, packs * lanes), jnp.bfloat16),
        compiler_params=pltpu.CompilerParams(vmem_limit_bytes=VMEM_BYTES),
        cost_estimate=pl.CostEstimate(
            flops=0, bytes_accessed=4 * slots * packs * lons * channels, transcendentals=0
        ),
    )(field)


def analyse_kernel(table_ref, x_ref, out_ref):
    sectors, slots, _, width = x_ref.shape
    total = None
    for j in range(sectors):
        cells = jnp.concatenate([x_ref[j, s] for s in range(slots)], axis=-1)
        part = jnp.dot(table_ref[j], cells, preferred_element_type=jnp.float32)
        total = part if total is None else total + part
    for s in range(slots):
        out_ref[0, s] = total[:, s * width : (s + 1) * width].astype(jnp.bfloat16)


def analyse(table, cells, bands):
    sectors, slots, lons, width = cells.shape
    rows = table.shape[1] // bands
    return pl.pallas_call(
        analyse_kernel,
        grid=(bands,),
        in_specs=[
            pl.BlockSpec((sectors, rows, lons), lambda d: (0, d, 0)),
            pl.BlockSpec((sectors, slots, lons, width), lambda d: (0, 0, 0, 0)),
        ],
        out_specs=pl.BlockSpec((1, slots, rows, width), lambda d: (d, 0, 0, 0)),
        out_shape=jax.ShapeDtypeStruct((bands, slots, rows, width), jnp.bfloat16),
        compiler_params=pltpu.CompilerParams(vmem_limit_bytes=VMEM_BYTES),
        cost_estimate=pl.CostEstimate(
            flops=2 * bands * rows * sectors * lons * slots * width,
            bytes_accessed=2 * (cells.size + table.size + bands * rows * slots * width),
            transcendentals=0,
        ),
    )(table, cells)


def disco_kernel(
    coef_ref, shift_ref, main_ref, prev_ref, next_ref, top_ref, bottom_ref,
    left_ref, right_ref, input_ref, weight_ref, grad_ref, taps_ref, ext_ref, spread_ref,
):
    step, steps = pl.program_id(0), pl.num_programs(0)
    rows, lons, channels = main_ref.shape

    @pl.when(step == 0)
    def _():
        taps_ref[...] = jnp.zeros_like(taps_ref)
        ext_ref[...] = jnp.zeros_like(ext_ref)

    for r in range(rows + 2):
        if r == 0:
            row = jnp.where(step == 0, top_ref[0].astype(jnp.float32), prev_ref[0].astype(jnp.float32))
        elif r == rows + 1:
            row = jnp.where(
                step == steps - 1, bottom_ref[0].astype(jnp.float32), next_ref[0].astype(jnp.float32)
            )
        else:
            row = main_ref[r - 1].astype(jnp.float32)
        ext_ref[r, 8 : 8 + lons] = row
        ext_ref[r, 7:8] = left_ref[step * rows + r]
        ext_ref[r, 8 + lons : 9 + lons] = right_ref[step * rows + r]
    for r in range(rows):
        cycle = step * rows + r
        for k, offset in enumerate((-1, 0, 1)):
            source = r + 1 - offset
            shift = shift_ref[cycle, k]
            picked = jnp.where(
                shift == 0,
                ext_ref[source, 8 : 8 + lons],
                jnp.where(
                    shift == 1, ext_ref[source, 7 : 7 + lons], ext_ref[source, 9 : 9 + lons]
                ),
            )
            spread_ref[:, k * channels : (k + 1) * channels] = (
                coef_ref[cycle, k] * picked
            ).astype(jnp.bfloat16)
        spread = spread_ref[...]
        grad_ref[r] = jnp.dot(spread, weight_ref[...], preferred_element_type=jnp.float32).astype(
            jnp.bfloat16
        )
        taps_ref[...] += lax.dot_general(
            input_ref[r], spread, (((0,), (0,)), ((), ())), preferred_element_type=jnp.float32
        )


def disco(coef, shifts, grad_out, top, bottom, left, right, block_input, weight):
    rows_here, lons, channels = grad_out.shape
    rows = largest_divisor(rows_here, 4)
    steps = rows_here // rows
    wide = weight.shape[0]
    whole = lambda shape: pl.BlockSpec(shape, lambda i: (0,) * len(shape))
    band = pl.BlockSpec((rows, lons, channels), lambda i: (i, 0, 0))
    return pl.pallas_call(
        disco_kernel,
        grid=(steps,),
        in_specs=[
            pl.BlockSpec(memory_space=pltpu.SMEM),
            pl.BlockSpec(memory_space=pltpu.SMEM),
            band,
            pl.BlockSpec((1, lons, channels), lambda i: (jnp.maximum(i * rows - 1, 0), 0, 0)),
            pl.BlockSpec(
                (1, lons, channels), lambda i: (jnp.minimum(i * rows + rows, rows_here - 1), 0, 0)
            ),
            whole(top.shape),
            whole(bottom.shape),
            whole(left.shape),
            whole(right.shape),
            band,
            whole(weight.shape),
        ],
        out_specs=[band, whole((channels, wide))],
        out_shape=[
            jax.ShapeDtypeStruct(grad_out.shape, jnp.bfloat16),
            jax.ShapeDtypeStruct((channels, wide), jnp.float32),
        ],
        scratch_shapes=[
            pltpu.VMEM((rows + 2, (lons + 9 + 15) // 8 * 8, channels), jnp.float32),
            pltpu.VMEM((lons, wide), jnp.bfloat16),
        ],
        compiler_params=pltpu.CompilerParams(vmem_limit_bytes=VMEM_BYTES),
        cost_estimate=pl.CostEstimate(
            flops=8 * rows_here * lons * channels * wide,
            bytes_accessed=6 * grad_out.size,
            transcendentals=0,
        ),
    )(coef, shifts, grad_out, grad_out, grad_out, top, bottom, left, right, block_input, weight)


def neighbours(first, last, axis):
    size = lax.axis_size(axis)
    up = [(i, (i + 1) % size) for i in range(size)]
    down = [(j, i) for i, j in up]
    return lax.ppermute(last, axis, up), lax.ppermute(first, axis, down)


def on_device(
    grad_out, block_input, leg_table, spec_coeff, spec_filter, cycle_weight, cycle_shift, tap_weight
):
    rows_here, lons_here, channels = grad_out.shape
    sectors, bands = lax.axis_size("lon"), lax.axis_size("lat")
    lon_total, cycle_total = lons_here * sectors, rows_here * bands
    orders_here = leg_table.shape[0]
    order_total = orders_here * bands
    lanes = channels // sectors

    top, bottom = neighbours(grad_out[:1], grad_out[-1:], "lat")

    def column(at):
        parts = [block[:, at : at + 1] for block in (top, grad_out, bottom)]
        return jnp.concatenate(parts, axis=0)

    left, right = neighbours(column(0), column(lons_here - 1), "lon")

    packs = largest_divisor(rows_here, max(1, 128 // lanes))
    chunks = largest_divisor(rows_here // packs, 4)
    slots = rows_here // (packs * chunks)
    field = grad_out.reshape(chunks, packs, slots, lons_here, channels)
    table = split_table(sectors, lons_here, order_total)
    packed = [pack(field, k, sectors) for k in range(chunks)]
    packed[0], left, right = lax.optimization_barrier((packed[0], left, right))

    pieces = []
    for k in range(chunks):
        cells = lax.all_to_all(packed[k], "lon", split_axis=0, concat_axis=0, tiled=True)
        part = analyse(table, cells, bands)
        part = lax.all_to_all(part, "lat", split_axis=0, concat_axis=0, tiled=True)
        part = part.reshape(bands, slots, orders_here, 2, packs, lanes)
        part = part.transpose(2, 0, 4, 1, 3, 5)
        pieces.append(part.reshape(orders_here, bands, packs * slots, 2 * lanes))

    cycle_start = lax.axis_index("lat") * rows_here
    weight_pad = jnp.pad(cycle_weight, ((1, 1), (0, 0)))
    shift_pad = jnp.pad(cycle_shift, ((1, 1), (0, 0)))

    def per_tap(padded):
        parts = [
            lax.dynamic_slice_in_dim(padded, cycle_start + 1 - offset, rows_here, 0)[:, k]
            for k, offset in enumerate((-1, 0, 1))
        ]
        return jnp.stack(parts, axis=-1)

    weight = tap_weight.transpose(0, 2, 1).reshape(-1, channels)
    input_grad, taps_part = disco(
        per_tap(weight_pad),
        per_tap(shift_pad),
        grad_out,
        top,
        bottom,
        left.astype(jnp.float32),
        right.astype(jnp.float32),
        block_input,
        weight,
    )
    taps_part = taps_part.reshape(channels, -1, channels).transpose(1, 0, 2)
    taps_grad = lax.psum(taps_part, ("lat", "lon")) / math.sqrt(cycle_total * lon_total)

    by_order = jnp.stack(pieces, axis=2).reshape(orders_here, cycle_total, 2 * lanes)
    degree = jnp.einsum("mla,man->lmn", leg_table, by_order, preferred_element_type=jnp.float32)
    degree = degree.reshape(-1, orders_here, 2, lanes)
    spec_grad = (degree * spec_filter[:, None, None, :]).astype(jnp.bfloat16)
    filter_part = jnp.sum(spec_coeff.astype(jnp.float32) * degree, axis=(1, 2)) / math.sqrt(
        2 * order_total
    )
    filter_grad = lax.psum(filter_part, "lat")
    return (spec_grad, filter_grad, input_grad, taps_grad)


def solution(mesh):
    in_specs = (
        P("lat", "lon", None),
        P("lat", "lon", None),
        P("lat", None, None),
        P(None, "lat", None, "lon"),
        P(None, "lon"),
        P(),
        P(),
        P(),
    )
    out_specs = (P(None, "lat", None, "lon"), P(None, "lon"), P("lat", "lon", None), P())
    return jax.shard_map(
        on_device, mesh=mesh, in_specs=in_specs, out_specs=out_specs, check_vma=False
    )
```

```python
import functools
import math

import jax
import jax.numpy as jnp
from jax import lax
from jax.experimental import pallas as pl
from jax.experimental.pallas import tpu as pltpu
from jax.sharding import PartitionSpec as P

VMEM_BYTES = 48 * 2**20


def largest_divisor(number, most):
    return max(d for d in range(1, most + 1) if number % d == 0)


def split_table(sectors, lons_here, mode_count):
    shape = (sectors, 2 * mode_count, lons_here)
    lon = lax.broadcasted_iota(jnp.int32, shape, 0) * lons_here + lax.broadcasted_iota(
        jnp.int32, shape, 2
    )
    row = lax.broadcasted_iota(jnp.int32, shape, 1)
    lon_count = sectors * lons_here
    phase = (lon * (row // 2) % lon_count).astype(jnp.float32) * (2.0 * math.pi / lon_count)
    value = jnp.where(row % 2 == 0, jnp.cos(phase), jnp.sin(phase)) / math.sqrt(lon_count)
    return value.astype(jnp.bfloat16)


def pack_kernel(groups, lanes, x_ref, out_ref):
    packs = x_ref.shape[1]
    for j in range(groups):
        parts = [x_ref[0, q, 0, :, j * lanes : (j + 1) * lanes] for q in range(packs)]
        out_ref[j, 0] = jnp.concatenate(parts, axis=-1)


def pack(field, chunk, groups):
    _, packs, slots, lons, channels = field.shape
    lanes = channels // groups
    return pl.pallas_call(
        functools.partial(pack_kernel, groups, lanes),
        grid=(slots,),
        in_specs=[pl.BlockSpec((1, packs, 1, lons, channels), lambda s: (chunk, 0, s, 0, 0))],
        out_specs=pl.BlockSpec((groups, 1, lons, packs * lanes), lambda s: (0, s, 0, 0)),
        out_shape=jax.ShapeDtypeStruct((groups, slots, lons, packs * lanes), jnp.bfloat16),
        compiler_params=pltpu.CompilerParams(vmem_limit_bytes=VMEM_BYTES),
        cost_estimate=pl.CostEstimate(
            flops=0, bytes_accessed=4 * slots * packs * lons * channels, transcendentals=0
        ),
    )(field)


def analyse_kernel(table_ref, x_ref, out_ref):
    sectors, slots, _, width = x_ref.shape
    total = None
    for j in range(sectors):
        cells = jnp.concatenate([x_ref[j, s] for s in range(slots)], axis=-1)
        part = jnp.dot(table_ref[j], cells, preferred_element_type=jnp.float32)
        total = part if total is None else total + part
    for s in range(slots):
        out_ref[0, s] = total[:, s * width : (s + 1) * width].astype(jnp.bfloat16)


def analyse(table, cells, bands):
    sectors, slots, lons, width = cells.shape
    rows = table.shape[1] // bands
    return pl.pallas_call(
        analyse_kernel,
        grid=(bands,),
        in_specs=[
            pl.BlockSpec((sectors, rows, lons), lambda d: (0, d, 0)),
            pl.BlockSpec((sectors, slots, lons, width), lambda d: (0, 0, 0, 0)),
        ],
        out_specs=pl.BlockSpec((1, slots, rows, width), lambda d: (d, 0, 0, 0)),
        out_shape=jax.ShapeDtypeStruct((bands, slots, rows, width), jnp.bfloat16),
        compiler_params=pltpu.CompilerParams(vmem_limit_bytes=VMEM_BYTES),
        cost_estimate=pl.CostEstimate(
            flops=2 * bands * rows * sectors * lons * slots * width,
            bytes_accessed=2 * (cells.size + table.size + bands * rows * slots * width),
            transcendentals=0,
        ),
    )(table, cells)


def disco_kernel(
    coef_ref, shift_ref, main_ref, prev_ref, next_ref, top_ref, bottom_ref,
    left_ref, right_ref, input_ref, weight_ref, grad_ref, taps_ref, ext_ref, spread_ref,
):
    step, steps = pl.program_id(0), pl.num_programs(0)
    rows, lons, channels = main_ref.shape

    @pl.when(step == 0)
    def _():
        taps_ref[...] = jnp.zeros_like(taps_ref)
        ext_ref[...] = jnp.zeros_like(ext_ref)

    for r in range(rows + 2):
        if r == 0:
            row = jnp.where(step == 0, top_ref[0].astype(jnp.float32), prev_ref[0].astype(jnp.float32))
        elif r == rows + 1:
            row = jnp.where(
                step == steps - 1, bottom_ref[0].astype(jnp.float32), next_ref[0].astype(jnp.float32)
            )
        else:
            row = main_ref[r - 1].astype(jnp.float32)
        ext_ref[r, 8 : 8 + lons] = row
        ext_ref[r, 7:8] = left_ref[step * rows + r]
        ext_ref[r, 8 + lons : 9 + lons] = right_ref[step * rows + r]
    for r in range(rows):
        cycle = step * rows + r
        for k, offset in enumerate((-1, 0, 1)):
            source = r + 1 - offset
            shift = shift_ref[cycle, k]
            picked = jnp.where(
                shift == 0,
                ext_ref[source, 8 : 8 + lons],
                jnp.where(
                    shift == 1, ext_ref[source, 7 : 7 + lons], ext_ref[source, 9 : 9 + lons]
                ),
            )
            spread_ref[:, k * channels : (k + 1) * channels] = (
                coef_ref[cycle, k] * picked
            ).astype(jnp.bfloat16)
        spread = spread_ref[...]
        grad_ref[r] = jnp.dot(spread, weight_ref[...], preferred_element_type=jnp.float32).astype(
            jnp.bfloat16
        )
        taps_ref[...] += lax.dot_general(
            input_ref[r], spread, (((0,), (0,)), ((), ())), preferred_element_type=jnp.float32
        )


def disco(coef, shifts, grad_out, top, bottom, left, right, block_input, weight):
    rows_here, lons, channels = grad_out.shape
    rows = largest_divisor(rows_here, 4)
    steps = rows_here // rows
    wide = weight.shape[0]
    whole = lambda shape: pl.BlockSpec(shape, lambda i: (0,) * len(shape))
    band = pl.BlockSpec((rows, lons, channels), lambda i: (i, 0, 0))
    return pl.pallas_call(
        disco_kernel,
        grid=(steps,),
        in_specs=[
            pl.BlockSpec(memory_space=pltpu.SMEM),
            pl.BlockSpec(memory_space=pltpu.SMEM),
            band,
            pl.BlockSpec((1, lons, channels), lambda i: (jnp.maximum(i * rows - 1, 0), 0, 0)),
            pl.BlockSpec(
                (1, lons, channels), lambda i: (jnp.minimum(i * rows + rows, rows_here - 1), 0, 0)
            ),
            whole(top.shape),
            whole(bottom.shape),
            whole(left.shape),
            whole(right.shape),
            band,
            whole(weight.shape),
        ],
        out_specs=[band, whole((channels, wide))],
        out_shape=[
            jax.ShapeDtypeStruct(grad_out.shape, jnp.bfloat16),
            jax.ShapeDtypeStruct((channels, wide), jnp.float32),
        ],
        scratch_shapes=[
            pltpu.VMEM((rows + 2, (lons + 9 + 15) // 8 * 8, channels), jnp.float32),
            pltpu.VMEM((lons, wide), jnp.bfloat16),
        ],
        compiler_params=pltpu.CompilerParams(vmem_limit_bytes=VMEM_BYTES),
        cost_estimate=pl.CostEstimate(
            flops=8 * rows_here * lons * channels * wide,
            bytes_accessed=6 * grad_out.size,
            transcendentals=0,
        ),
    )(coef, shifts, grad_out, grad_out, grad_out, top, bottom, left, right, block_input, weight)


def neighbours(first, last, axis):
    size = lax.axis_size(axis)
    up = [(i, (i + 1) % size) for i in range(size)]
    down = [(j, i) for i, j in up]
    return lax.ppermute(last, axis, up), lax.ppermute(first, axis, down)


def swap_bands(blocks, axis):
    size = lax.axis_size(axis)
    me = lax.axis_index(axis)
    by_distance = [lax.dynamic_index_in_dim(blocks, me, 0, keepdims=True)]
    for step in range(1, size):
        block = lax.dynamic_index_in_dim(blocks, lax.rem(me + step, size), 0, keepdims=True)
        pairs = [(i, (i + step) % size) for i in range(size)]
        by_distance.append(lax.ppermute(block, axis, pairs))
    stacked = jnp.concatenate(by_distance, axis=0)
    ordered = [
        lax.dynamic_index_in_dim(stacked, lax.rem(me - b + size, size), 0, keepdims=True)
        for b in range(size)
    ]
    return jnp.concatenate(ordered, axis=0)


def on_device(
    grad_out, block_input, leg_table, spec_coeff, spec_filter, cycle_weight, cycle_shift, tap_weight
):
    rows_here, lons_here, channels = grad_out.shape
    sectors, bands = lax.axis_size("lon"), lax.axis_size("lat")
    lon_total, cycle_total = lons_here * sectors, rows_here * bands
    orders_here = leg_table.shape[0]
    order_total = orders_here * bands
    lanes = channels // sectors

    top, bottom = neighbours(grad_out[:1], grad_out[-1:], "lat")

    def column(at):
        parts = [block[:, at : at + 1] for block in (top, grad_out, bottom)]
        return jnp.concatenate(parts, axis=0)

    left, right = neighbours(column(0), column(lons_here - 1), "lon")

    packs = largest_divisor(rows_here, max(1, 128 // lanes))
    chunks = largest_divisor(rows_here // packs, 4)
    slots = rows_here // (packs * chunks)
    field = grad_out.reshape(chunks, packs, slots, lons_here, channels)
    table = split_table(sectors, lons_here, order_total)
    packed = [pack(field, k, sectors) for k in range(chunks)]

    cycle_start = lax.axis_index("lat") * rows_here
    weight_pad = jnp.pad(cycle_weight, ((1, 1), (0, 0)))
    shift_pad = jnp.pad(cycle_shift, ((1, 1), (0, 0)))

    def per_tap(padded):
        parts = [
            lax.dynamic_slice_in_dim(padded, cycle_start + 1 - offset, rows_here, 0)[:, k]
            for k, offset in enumerate((-1, 0, 1))
        ]
        return jnp.stack(parts, axis=-1)

    weight = tap_weight.transpose(0, 2, 1).reshape(-1, channels)
    input_grad, taps_part = disco(
        per_tap(weight_pad),
        per_tap(shift_pad),
        grad_out,
        top,
        bottom,
        left.astype(jnp.float32),
        right.astype(jnp.float32),
        block_input,
        weight,
    )

    def reduce_taps(part):
        part = part.reshape(channels, -1, channels).transpose(1, 0, 2)
        return lax.psum(part, ("lat", "lon")) / math.sqrt(cycle_total * lon_total)

    barrier = lax.optimization_barrier
    pieces = []
    previous = None
    for k in range(chunks):
        sent = packed[k]
        if previous is not None:
            sent, previous = barrier((sent, previous))
        if k == 2:
            sent, input_grad, taps_part = barrier((sent, input_grad, taps_part))
        if k == 3:
            sent, pieces[0] = barrier((sent, pieces[0]))
        cells = lax.all_to_all(sent, "lon", split_axis=0, concat_axis=0, tiled=True)
        previous = cells
        if k == 2:
            taps_grad = reduce_taps(taps_part)
        if k == 3:
            cells, pieces[1], pieces[2], taps_grad = barrier(
                (cells, pieces[1], pieces[2], taps_grad)
            )
        part = swap_bands(analyse(table, cells, bands), "lat")
        part = part.reshape(bands, slots, orders_here, 2, packs, lanes)
        part = part.transpose(2, 0, 4, 1, 3, 5)
        pieces.append(part.reshape(orders_here, bands, packs * slots, 2 * lanes))
    if chunks < 3:
        taps_grad = reduce_taps(taps_part)

    by_order = jnp.stack(pieces, axis=2).reshape(orders_here, cycle_total, 2 * lanes)
    degree = jnp.einsum("mla,man->lmn", leg_table, by_order, preferred_element_type=jnp.float32)
    degree = degree.reshape(-1, orders_here, 2, lanes)
    spec_grad = (degree * spec_filter[:, None, None, :]).astype(jnp.bfloat16)
    filter_part = jnp.sum(spec_coeff.astype(jnp.float32) * degree, axis=(1, 2)) / math.sqrt(
        2 * order_total
    )
    filter_grad = lax.psum(filter_part, "lat")
    return (spec_grad, filter_grad, input_grad, taps_grad)


def solution(mesh):
    in_specs = (
        P("lat", "lon", None),
        P("lat", "lon", None),
        P("lat", None, None),
        P(None, "lat", None, "lon"),
        P(None, "lon"),
        P(),
        P(),
        P(),
    )
    out_specs = (P(None, "lat", None, "lon"), P(None, "lon"), P("lat", "lon", None), P())
    return jax.shard_map(
        on_device, mesh=mesh, in_specs=in_specs, out_specs=out_specs, check_vma=False
    )
```
